256 devices in a mesh: ctx: 32 (over z_lo, y, x), head: 8 (over z_hi, core).
Axes of the slice: x: 4, y: 4, z: 8 (z_hi: 4, z_lo: 2; z = z_hi * 2 + z_lo), core: 2. Of those that a mesh axis runs over, the one named last changes fastest.
Arguments:
- queries: bfloat16 [16384, 4096], P('ctx', 'head'), may hold values from -240 to 240
- key_rows: bfloat16 [16384, 4, 128], P('ctx'), may hold values from -8 to 8
- value_vectors: bfloat16 [16384, 4, 128], P('ctx'), may hold values from -6 to 6
- out_weight: bfloat16 [4096, 2048], P('head'), may hold values from -0.125 to 0.125
- doc_start: int32 [128], P('ctx'), may hold values from 0 to 127, as said below
- block_list: int32 [32, 35], P('ctx'), may hold values from -1 to 127, as said below
Outputs:
- projected: bfloat16 [16384, 2048], P('ctx', 'head')
The draws below stay inside these ranges and needn't reach their ends.
Inputs may be any that keep to these rules, and one draw needn't show every extreme that they name: `doc_start`: documents begin on block boundaries and are 1 to 32 blocks long, one of them exactly 32; the last block begins a document of its own. `block_list`: row r holds, ascending, every block from the document start of block r * 4 through block (r + 1) * 4 - 1, and -1 in the slots after.
All inputs are finite; a program needn't handle non-finite values.
Results may differ from the reference program's by a relative error of at most 0.018.
Values may be sent and summed in bfloat16 or wider, within the bound.
No kernel may reach another device: no remote copies, remote signals or barrier semaphores. Data moves between devices by JAX's collectives and lax.ppermute only.
A program may use at most 64 MiB of HBM per device.

```python
import math
import jax
import jax.numpy as jnp
from jax import lax

D = 2048
QUERY_HEADS = 32
KEY_VALUE_HEADS = 4
HEAD_WIDTH = 128
BLK = 128
DOC_BLOCKS = 32
TOKENS_PER_SHARD = 512
PACKED_TOKENS = 16384
NBLK = 128
BLK_DEV = 4
REACH = 8
LIST = 35
N_CTX = 32
N_HEAD = 8


def doc_table(key):
    doc_key = jax.random.fold_in(key, 7)
    lengths = jax.random.randint(jax.random.fold_in(doc_key, 1), (NBLK,), 1, DOC_BLOCKS + 1)
    long_place = jax.random.randint(jax.random.fold_in(doc_key, 2), (), 0, 2)
    block_ids = jnp.arange(NBLK, dtype=jnp.int32)
    lengths = jnp.where(block_ids == long_place, DOC_BLOCKS, lengths).astype(jnp.int32)
    doc_starts = jnp.cumsum(lengths) - lengths
    doc_marks = jnp.zeros((NBLK,), jnp.int32).at[doc_starts].set(1, mode='drop')
    doc_marks = jnp.where(block_ids == NBLK - 1, 1, doc_marks)
    return lax.cummax(jnp.where(doc_marks == 1, block_ids, 0), axis=0).astype(jnp.int32)


def draw_doc_start(key, part):
    return doc_table(key)


def draw_block_list(key, part):
    starts_table = doc_table(key)
    readers = NBLK // BLK_DEV
    reader_ids = jnp.arange(readers, dtype=jnp.int32)
    first_blocks = starts_table[reader_ids * BLK_DEV]
    last_blocks = reader_ids * BLK_DEV + BLK_DEV - 1
    block_ids = first_blocks[:, None] + jnp.arange(LIST, dtype=jnp.int32)[None, :]
    return jnp.where(block_ids <= last_blocks[:, None], block_ids, -1).astype(jnp.int32)


def key_matrix(key):
    gaussian_sample = jax.random.normal(jax.random.fold_in(key, 11), (PACKED_TOKENS, KEY_VALUE_HEADS, HEAD_WIDTH), jnp.float32)
    drawn = jnp.clip(gaussian_sample, -6.0, 6.0)
    return drawn


def draw_key_rows(key, part):
    return key_matrix(key).astype(jnp.bfloat16)


def draw_queries(key, part):
    gaussian_sample = jax.random.normal(jax.random.fold_in(key, 13), (PACKED_TOKENS, QUERY_HEADS * HEAD_WIDTH), jnp.float32)
    drawn = jnp.clip(gaussian_sample, -6.0, 6.0)
    return drawn.astype(jnp.bfloat16)


def strengthened(values, key, source, target, parts, factor):
    def block_of(position):
        return (jnp.arange(values.shape[position]) // (values.shape[position] // parts)).reshape((-1,) + (1,) * (values.ndim - 1 - position))

    one_side = jax.random.permutation(key, parts)[block_of(target)]
    second = (block_of(target) + parts // 2) % parts
    return jnp.where((block_of(source) == one_side) | (block_of(source) == second), factor * values, values)


def levels(key, extent, pieces, least, top_value):
    factor_of, own = 1.0, jax.random.fold_in(key, 6)
    for axis_at, blocks in pieces:
        steps = jnp.exp(jax.random.uniform(jax.random.fold_in(own, axis_at), (blocks,), jnp.float32, least / len(pieces), top_value / len(pieces)))
        factor_of = factor_of * jnp.repeat(steps, extent[axis_at] // blocks).reshape([-1 if axis == axis_at else 1 for axis in range(len(extent))])
    return factor_of


def noise(rng, dims, width, bound, pieces=(), held_as=jnp.bfloat16):
    gain = levels(rng, dims, pieces, -0.22, 0.18) if pieces else 1.0
    result = jax.random.normal(rng, dims, jnp.float32) * width * gain
    return jnp.minimum(jnp.maximum(result, -bound), bound).astype(held_as)


def noise_with(own_key, shape, deviation, bound, split, heavy, kind=jnp.bfloat16):
    entries = deviation * jax.random.normal(own_key, shape, jnp.float32)
    if split:
        entries = entries * levels(own_key, shape, split, -0.22, 0.18)
    return jnp.clip(strengthened(entries, jax.random.fold_in(own_key, 3), *heavy), -bound, bound).astype(kind)


def setup_inputs(seed: int = 0) -> dict:
    key_of = jax.random.split(jax.random.key(seed), 7)
    queries = draw_queries(jax.random.fold_in(key_of[6], 71), 0)
    key_rows = draw_key_rows(jax.random.fold_in(key_of[6], 71), 0)
    value_vectors = noise(key_of[2], (PACKED_TOKENS, KEY_VALUE_HEADS, HEAD_WIDTH), 1.0, 6.0, ((0, 32),))
    out_weight = noise_with(key_of[3], (QUERY_HEADS * HEAD_WIDTH, D), (QUERY_HEADS * HEAD_WIDTH) ** -0.5, 0.125, ((0, 8),), (0, 1, 8, 2.0))
    doc_start = draw_doc_start(jax.random.fold_in(key_of[6], 71), 0)
    block_list = draw_block_list(jax.random.fold_in(key_of[6], 71), 0)
    return {"queries": queries, "key_rows": key_rows, "value_vectors": value_vectors, "out_weight": out_weight, "doc_start": doc_start, "block_list": block_list}


NEGATIVE_FILL = -1e+30

def reference(queries, key_rows, value_vectors, out_weight, doc_start, block_list):
    heads_per_group = QUERY_HEADS // KEY_VALUE_HEADS
    key_span = (REACH + 1) * TOKENS_PER_SHARD
    score_scale = 1.0 / math.sqrt(HEAD_WIDTH)
    doc_tokens = jnp.repeat(doc_start, BLK)

    def one_reader(reader):
        key_first = (jnp.maximum(reader - REACH, 0) * TOKENS_PER_SHARD).astype(jnp.int32)
        query_first = (reader * TOKENS_PER_SHARD).astype(jnp.int32)
        grouped_queries = lax.dynamic_slice_in_dim(queries, query_first, TOKENS_PER_SHARD, 0).astype(jnp.float32)
        grouped_queries = grouped_queries.reshape(TOKENS_PER_SHARD, KEY_VALUE_HEADS, heads_per_group, HEAD_WIDTH)
        near_keys = lax.dynamic_slice_in_dim(key_rows, key_first, key_span, 0).astype(jnp.float32)
        near_values = lax.dynamic_slice_in_dim(value_vectors, key_first, key_span, 0).astype(jnp.float32)
        query_pos = query_first + jnp.arange(TOKENS_PER_SHARD, dtype=jnp.int32)
        key_pos = key_first + jnp.arange(key_span, dtype=jnp.int32)
        query_docs = lax.dynamic_slice_in_dim(doc_tokens, query_first, TOKENS_PER_SHARD, 0)
        listed = block_list[reader]
        key_block = key_pos // BLK
        in_list = jnp.any(listed[None, :] == key_block[:, None], axis=1)
        allowed = (key_pos[None, :] <= query_pos[:, None]) & (key_block[None, :] >= query_docs[:, None]) & in_list[None, :]
        scores = jnp.einsum('tkgd,skd->kgts', grouped_queries, near_keys) * score_scale
        scores = jnp.where(allowed, scores, NEGATIVE_FILL)
        row_max = lax.optimization_barrier(jnp.max(scores, axis=-1, keepdims=True))
        weights = jnp.where(allowed, jnp.exp(scores - row_max), 0.0)
        weight_sum = lax.optimization_barrier(jnp.sum(weights, axis=-1))
        rounded = lax.optimization_barrier(weights.astype(jnp.bfloat16)).astype(jnp.float32)
        head_mix = jnp.einsum('kgts,skd->kgtd', rounded, near_values) / weight_sum[..., None]
        return head_mix.transpose(2, 0, 1, 3).reshape(TOKENS_PER_SHARD, QUERY_HEADS * HEAD_WIDTH).astype(jnp.bfloat16)
    heads_out = lax.map(one_reader, jnp.arange(N_CTX, dtype=jnp.int32)).reshape(PACKED_TOKENS, QUERY_HEADS * HEAD_WIDTH)
    group_width = QUERY_HEADS // N_HEAD * HEAD_WIDTH
    summed = jnp.zeros((PACKED_TOKENS, D), jnp.float32)
    for group_index in range(N_HEAD):
        lower = group_index * group_width
        term = jnp.dot(heads_out[:, lower:lower + group_width], out_weight[lower:lower + group_width], preferred_element_type=jnp.float32)
        summed = summed + lax.optimization_barrier(term.astype(jnp.bfloat16)).astype(jnp.float32)
    return summed.astype(jnp.bfloat16)
```

```python
import functools
import math

import jax
import jax.numpy as jnp
from jax import lax
from jax.experimental import pallas as pl
from jax.experimental.pallas import tpu as pltpu
from jax.sharding import PartitionSpec as P

HEAD_WIDTH = 128
BLK = 128
DOC_BLOCKS = 32
REACH = 8
SHARD = 512
WINDOW = DOC_BLOCKS * BLK
SPAN = (REACH + 1) * SHARD
KEY_TILE = 2048
NEG = -1e30
EXP_SCALE = math.log2(math.e) / math.sqrt(HEAD_WIDTH)
AXES = ("ctx", "head")
SHIFTS = ((1, 5), (2, 6), (3, 7), (4, 8))


def ctx_head_pairs(n_ctx, n_head, route):
    pairs = []
    for c in range(n_ctx):
        for h in range(n_head):
            target = route(c, h)
            if target is not None:
                pairs.append((c * n_head + h, target[0] * n_head + target[1]))
    return pairs


def fetch(block, n_ctx, n_head, by_core):
    def route(c, h):
        d = c + by_core[h % 2]
        return (d, h) if d < n_ctx else None

    return lax.ppermute(block, AXES, ctx_head_pairs(n_ctx, n_head, route))


def swap_cores(block, n_ctx, n_head):
    return lax.ppermute(
        block, AXES, ctx_head_pairs(n_ctx, n_head, lambda c, h: (c, h ^ 1))
    )


def send_piece(block, n_ctx, n_head, dz, dc):
    def route(c, h):
        return (c, (((h // 2 + dz) % (n_head // 2)) * 2) + ((h % 2) ^ dc))

    return lax.ppermute(block, AXES, ctx_head_pairs(n_ctx, n_head, route))


def dot_t(a, b):
    return lax.dot_general(
        a, b, (((1,), (1,)), ((), ())), preferred_element_type=jnp.float32
    )


def attend_kernel(doc_ref, list_ref, q_ref, rq_ref, own_ref, *rest):
    n_sh = len(SHIFTS)
    mine, theirs = rest[:n_sh], rest[n_sh : 2 * n_sh]
    w_ref, rw_ref = rest[2 * n_sh : 2 * n_sh + 2]
    outs = rest[2 * n_sh + 2 : 2 * n_sh + 10]
    kx, vx, qs, ws, ho, bias, sem = rest[2 * n_sh + 10 :]
    ctx = lax.axis_index("ctx")
    head = lax.axis_index("head")
    core = lax.rem(head, 2)
    z = lax.div(head, 2)

    copies = []

    def start(src, dst):
        c = pltpu.make_async_copy(src, dst, sem.at[len(copies)])
        c.start()
        copies.append(c)

    def load_shard(ref, distance):
        row = pl.multiple_of((REACH - distance) * SHARD, SHARD)
        start(ref.at[:SHARD], kx.at[pl.ds(row, SHARD)])
        start(ref.at[SHARD:], vx.at[pl.ds(row, SHARD), pl.ds(0, HEAD_WIDTH)])

    half = pl.multiple_of(core * 256, 256)
    start(q_ref.at[pl.ds(half, 256)], qs.at[:, pl.ds(0, 512)])
    start(rq_ref.at[pl.ds(half, 256)], qs.at[:, pl.ds(512, 512)])
    load_shard(own_ref, 0)
    for (d0, d1), a, b in zip(SHIFTS, mine, theirs):
        load_shard(a, jnp.where(core == 0, d0, d1))
        load_shard(b, jnp.where(core == 0, d1, d0))
    start(w_ref, ws.at[pl.ds(0, 512)])
    start(rw_ref, ws.at[pl.ds(512, 512)])
    vx[:, HEAD_WIDTH:] = jnp.ones((SPAN, HEAD_WIDTH), jnp.bfloat16)

    list_first = list_ref[0, 0]
    list_last = lax.fori_loop(
        0, list_ref.shape[1], lambda i, m: jnp.maximum(m, list_ref[0, i]), -1
    )
    base = (ctx - REACH) * (SHARD // BLK)
    for c in copies[:-2]:
        c.wait()

    def block(ii, carry):
        local = core * 2 + ii
        first = local + 1
        win = pl.multiple_of(first * BLK, BLK)
        row = pl.multiple_of(ii * BLK, BLK)
        lo = jnp.maximum(doc_ref[local], list_first) - base - first
        hi = jnp.minimum(DOC_BLOCKS - 1, list_last - base - first)
        col_block = lax.broadcasted_iota(jnp.int32, (8, WINDOW), 1) // BLK
        bias[...] = jnp.where((col_block >= lo) & (col_block <= hi), 0.0, NEG)
        causal = lax.broadcasted_iota(jnp.int32, (BLK, BLK), 1) <= (
            lax.broadcasted_iota(jnp.int32, (BLK, BLK), 0)
        )
        for g in range(8):
            q = qs[pl.ds(row, BLK), g * HEAD_WIDTH : (g + 1) * HEAD_WIDTH]
            m = None
            for t in range(0, WINDOW, KEY_TILE):
                s = dot_t(q, kx[pl.ds(win + t, KEY_TILE), :])
                s = s + bias[0:1, t : t + KEY_TILE]
                if t + KEY_TILE == WINDOW:
                    s = jnp.concatenate(
                        [s[:, :-BLK], jnp.where(causal, s[:, -BLK:], NEG)], axis=1
                    )
                top = jnp.max(s, axis=1, keepdims=True)
                m_new = top if m is None else jnp.maximum(m, top)
                p = jnp.exp2((s - m_new) * EXP_SCALE).astype(jnp.bfloat16)
                pv = jnp.dot(
                    p,
                    vx[pl.ds(win + t, KEY_TILE), :],
                    preferred_element_type=jnp.float32,
                )
                if m is None:
                    acc = pv
                else:
                    acc = acc * jnp.exp2((m - m_new) * EXP_SCALE) + pv
                m = m_new
            o = acc[:, :HEAD_WIDTH] / acc[:, HEAD_WIDTH:]
            ho[pl.ds(row, BLK), g * HEAD_WIDTH : (g + 1) * HEAD_WIDTH] = o.astype(
                jnp.bfloat16
            )
        return carry

    lax.fori_loop(0, 2, block, 0)
    for c in copies[-2:]:
        c.wait()
    for p in range(8):
        dz, dc = p // 2, p % 2
        target = lax.rem(z + dz, 4) * 2 + lax.rem(core + dc, 2)
        col = pl.multiple_of(target * 256, 256)
        outs[p][...] = jnp.dot(
            ho[...], ws[:, pl.ds(col, 256)], preferred_element_type=jnp.float32
        ).astype(jnp.bfloat16)


def attend(doc_start, block_list, q, rq, own, mine, theirs, w, rw):
    smem = pl.BlockSpec(memory_space=pltpu.SMEM)
    anyspec = pl.BlockSpec(memory_space=pl.ANY)
    vmem = pl.BlockSpec(memory_space=pltpu.VMEM)
    n_arrays = 3 + len(mine) + len(theirs) + 2
    return pl.pallas_call(
        attend_kernel,
        out_shape=[jax.ShapeDtypeStruct((256, 256), jnp.bfloat16)] * 8,
        in_specs=[smem, smem] + [anyspec] * n_arrays,
        out_specs=[vmem] * 8,
        scratch_shapes=[
            pltpu.VMEM((SPAN, HEAD_WIDTH), jnp.bfloat16),
            pltpu.VMEM((SPAN, 2 * HEAD_WIDTH), jnp.bfloat16),
            pltpu.VMEM((256, 1024), jnp.bfloat16),
            pltpu.VMEM((1024, 2048), jnp.bfloat16),
            pltpu.VMEM((256, 1024), jnp.bfloat16),
            pltpu.VMEM((8, WINDOW), jnp.float32),
            pltpu.SemaphoreType.DMA((22,)),
        ],
        compiler_params=pltpu.CompilerParams(vmem_limit_bytes=40 * 2**20),
        cost_estimate=pl.CostEstimate(
            flops=6 * 10**9, bytes_accessed=8 * 2**20, transcendentals=9 * 10**6
        ),
        name="attend",
    )(doc_start, block_list, q, rq, own, *mine, *theirs, w, rw)


def on_device(n_ctx, n_head, queries, key_rows, value_vectors, out_weight, doc_start, block_list):
    head = lax.axis_index("head")
    core = head % 2
    z = head // 2
    swap = functools.partial(swap_cores, n_ctx=n_ctx, n_head=n_head)
    own_k = lax.dynamic_index_in_dim(key_rows, z, 1, keepdims=False)
    own_v = lax.dynamic_index_in_dim(value_vectors, z, 1, keepdims=False)
    own = jnp.concatenate([own_k, own_v], axis=0)
    mine = [fetch(own, n_ctx, n_head, s) for s in SHIFTS]
    rq = swap(queries)
    rw = swap(out_weight)
    theirs = [swap(a) for a in mine]
    pieces = attend(
        doc_start, block_list, queries, rq, own, mine, theirs, out_weight, rw
    )
    got = []
    for p in range(8):
        dz, dc = p // 2, p % 2
        got.append(
            pieces[p]
            if p == 0
            else send_piece(pieces[p], n_ctx, n_head, dz, dc)
        )
    same = sum(g.astype(jnp.float32) for g in got[0::2]).astype(jnp.bfloat16)
    other = sum(g.astype(jnp.float32) for g in got[1::2]).astype(jnp.bfloat16)
    return jnp.where(
        core == 0,
        jnp.concatenate([same, other], axis=0),
        jnp.concatenate([other, same], axis=0),
    )


def solution(mesh):
    n_ctx, n_head = mesh.shape["ctx"], mesh.shape["head"]
    return jax.shard_map(
        functools.partial(on_device, n_ctx, n_head),
        mesh=mesh,
        in_specs=(
            P("ctx", "head"),
            P("ctx", None, None),
            P("ctx", None, None),
            P("head", None),
            P("ctx"),
            P("ctx", None),
        ),
        out_specs=P("ctx", "head"),
        check_vma=False,
    )
```

```python
import functools
import math

import jax
import jax.numpy as jnp
from jax import lax
from jax.experimental import pallas as pl
from jax.experimental.pallas import tpu as pltpu
from jax.sharding import PartitionSpec as P

HEAD_WIDTH = 128
BLK = 128
DOC_BLOCKS = 32
REACH = 8
SHARD = 512
HALF = 256
PIECE = 256
NEG = -1e30
EXP_SCALE = math.log2(math.e) / math.sqrt(HEAD_WIDTH)
AXES = ("ctx", "head")
X_CHIPS = 4
GRANT = 40 * 2**20


def ctx_head_pairs(n_ctx, n_head, route):
    pairs = []
    for c in range(n_ctx):
        for h in range(n_head):
            target = route(c, h)
            if target is not None:
                pairs.append((c * n_head + h, target[0] * n_head + target[1]))
    return pairs


def send(block, n_ctx, n_head, route):
    return lax.ppermute(block, AXES, ctx_head_pairs(n_ctx, n_head, route))


def to_later_rows(n_ctx):
    def route(c, h):
        d = c + 4 + 4 * (h % 2)
        return (d, h) if d < n_ctx else None

    return route


def turned(c, by):
    return c - c % X_CHIPS + (c + by) % X_CHIPS


def beside(c, h):
    return (turned(c, 1 if h % 2 == 0 else 3), h)


def across(c, h):
    return (turned(c, 2), h)


def other_core(c, h):
    return (c, h ^ 1)


def along_z(n_head):
    return lambda c, h: (c, (h + (2 if h % 2 == 0 else -2)) % n_head)


def dot_t(a, b):
    return lax.dot_general(
        a, b, (((1,), (1,)), ((), ())), preferred_element_type=jnp.float32
    )


def position():
    head = lax.axis_index("head")
    return lax.axis_index("ctx"), lax.div(head, 2), lax.rem(head, 2)


class Copies:
    def __init__(self, sem):
        self.sem, self.started = sem, []

    def start(self, src, dst):
        c = pltpu.make_async_copy(src, dst, self.sem.at[len(self.started)])
        c.start()
        self.started.append(c)

    def wait(self, first=0, last=None):
        for c in self.started[first:last]:
            c.wait()


def last_listed(list_ref):
    last = list_ref[0, 0]
    for i in range(1, list_ref.shape[1]):
        last = jnp.maximum(last, list_ref[0, i])
    return last


def block_range(doc_ref, list_ref, list_last, ctx, local):
    lo = jnp.maximum(doc_ref[local], list_ref[0, 0])
    hi = jnp.minimum(ctx * (SHARD // BLK) + local, list_last)
    return lo, hi


def write_bias(bias, ctx, distances, lo, hi):
    for j, d in enumerate(distances):
        block = (ctx - d) * (SHARD // BLK) + (
            lax.broadcasted_iota(jnp.int32, (bias.shape[0], SHARD), 1) // BLK
        )
        bias[:, j * SHARD : (j + 1) * SHARD] = jnp.where(
            (block >= lo) & (block <= hi), 0.0, NEG
        )


def load_shard(copies, ref, first, kx, vx, row):
    copies.start(ref.at[pl.ds(first, SHARD)], kx.at[pl.ds(row, SHARD)])
    copies.start(
        ref.at[pl.ds(first + SHARD, SHARD)],
        vx.at[pl.ds(row, SHARD), pl.ds(0, HEAD_WIDTH)],
    )


def softmax_tile(q, k, v, mask, m, acc):
    s = dot_t(q, k) + mask
    top = jnp.max(s, axis=1, keepdims=True)
    m_new = top if m is None else jnp.maximum(m, top)
    p = jnp.exp2((s - m_new) * EXP_SCALE).astype(jnp.bfloat16)
    pv = jnp.dot(p, v, preferred_element_type=jnp.float32)
    if m is not None:
        pv = acc * jnp.exp2((m - m_new) * EXP_SCALE) + pv
    return m_new, pv


def head_columns(g):
    return slice(g * HEAD_WIDTH, (g + 1) * HEAD_WIDTH)


def turn_distances(core):
    return [jnp.where(core == 0, a, b) for a, b in ((1, 3), (5, 7), (2, 6))]


def load_queries(copies, q_ref, rq_ref, row, rows, qs):
    at = pl.multiple_of(row, BLK)
    copies.start(q_ref.at[pl.ds(at, rows)], qs.at[:, pl.ds(0, 512)])
    copies.start(rq_ref.at[pl.ds(at, rows)], qs.at[:, pl.ds(512, 512)])


def near_kernel(doc_ref, list_ref, q_ref, rq_ref, own, mine, theirs, *rest):
    acc_ref, ml_ref, kx, vx, qs, mask, sem = rest
    ctx, z, core = position()
    copies = Copies(sem)
    load_queries(copies, q_ref, rq_ref, core * HALF, HALF, qs)
    load_shard(copies, own, 0, kx, vx, 0)
    load_shard(copies, mine, 0, kx, vx, pl.multiple_of((1 + core) * SHARD, SHARD))
    load_shard(copies, theirs, 0, kx, vx, pl.multiple_of((2 - core) * SHARD, SHARD))
    vx[:, HEAD_WIDTH:] = jnp.ones((vx.shape[0], HEAD_WIDTH), jnp.bfloat16)
    lane = lax.broadcasted_iota(jnp.int32, (BLK, HEAD_WIDTH), 1)
    list_last = last_listed(list_ref)

    def write_mask(ii):
        local = core * 2 + ii
        lo, hi = block_range(doc_ref, list_ref, list_last, ctx, local)
        write_bias(mask, ctx, (0, 4, 8), lo, hi)
        col = lax.broadcasted_iota(jnp.int32, (BLK, SHARD), 1)
        at = lax.broadcasted_iota(jnp.int32, (BLK, SHARD), 0) + local * BLK
        mask[:, :SHARD] = jnp.where(col <= at, mask[:, :SHARD], NEG)

    def block(ii, carry):
        rows = pl.ds(pl.multiple_of(ii * BLK, BLK), BLK)
        ml = jnp.zeros((BLK, HEAD_WIDTH), jnp.float32)
        for g in range(8):
            q = qs[rows, head_columns(g)]
            m, acc = softmax_tile(q, kx[...], vx[...], mask[...], None, None)
            acc_ref[rows, head_columns(g)] = acc[:, :HEAD_WIDTH]
            ml = jnp.where(lane == g, m, ml)
            ml = jnp.where(lane == 8 + g, acc[:, HEAD_WIDTH:], ml)
        ml_ref[rows, :] = ml

        @pl.when(ii == 0)
        def _():
            write_mask(1)

        return carry

    write_mask(0)
    copies.wait()
    lax.fori_loop(0, 2, block, 0)


def joined(acc_ref, ml_ref, rows, g):
    l_in = jnp.broadcast_to(ml_ref[rows, 8 + g : 9 + g], (BLK, HEAD_WIDTH))
    acc = jnp.concatenate([acc_ref[rows, head_columns(g)], l_in], axis=1)
    return ml_ref[rows, g : g + 1], acc


def far_kernel(doc_ref, list_ref, q_ref, rq_ref, *rest):
    turns, (acc_in, ml_in, ho) = rest[:4], rest[4:7]
    kx, vx, qs, bias, acc_s, ml_s, sem = rest[7:]
    ctx, z, core = position()
    copies = Copies(sem)
    for i in range(2):
        at = 3 * i * SHARD
        load_shard(copies, turns[2 * i], 0, kx, vx, at)
        load_shard(copies, turns[2 * i], 2 * SHARD, kx, vx, at + SHARD)
        load_shard(copies, turns[2 * i + 1], 0, kx, vx, at + 2 * SHARD)
    load_queries(copies, q_ref, rq_ref, core * HALF, HALF, qs)
    copies.start(acc_in, acc_s)
    copies.start(ml_in, ml_s)
    vx[:, HEAD_WIDTH:] = jnp.ones((vx.shape[0], HEAD_WIDTH), jnp.bfloat16)
    distances = turn_distances(core) + turn_distances(1 - core)
    list_last = last_listed(list_ref)
    for ii in range(2):
        lo, hi = block_range(doc_ref, list_ref, list_last, ctx, core * 2 + ii)
        write_bias(bias.at[ii], ctx, distances, lo, hi)
    copies.wait()

    def block(ii, carry):
        rows = pl.ds(pl.multiple_of(ii * BLK, BLK), BLK)
        for g in range(8):
            q = qs[rows, head_columns(g)]
            m, acc = joined(acc_s, ml_s, rows, g)
            _, acc = softmax_tile(q, kx[...], vx[...], bias[ii, 0:1, :], m, acc)
            o = acc[:, :HEAD_WIDTH] / acc[:, HEAD_WIDTH:]
            ho[rows, head_columns(g)] = o.astype(jnp.bfloat16)
        return carry

    lax.fori_loop(0, 2, block, 0)

def project_kernel(ho_ref, got_ref, w_ref, rw_ref, *rest):
    outs = rest[:4]
    ho, ws, sem = rest[4:]
    ctx, z, core = position()
    copies = Copies(sem)
    dz = jnp.where(core == 0, 1, 3)
    wanted = ((2, core), (dz, 1 - core), (dz, core), (0, core))
    mine = pl.ds(pl.multiple_of(core * HALF, HALF), HALF)
    theirs = pl.ds(pl.multiple_of((1 - core) * HALF, HALF), HALF)
    copies.start(ho_ref, ho.at[mine])
    copies.start(got_ref.at[:, pl.ds(0, 512)], ho.at[theirs, pl.ds(512, 512)])
    copies.start(got_ref.at[:, pl.ds(512, 512)], ho.at[theirs, pl.ds(0, 512)])
    for i, (away, part) in enumerate(wanted):
        target = lax.rem(z + away, 4) * 2 + part
        col = pl.ds(pl.multiple_of(target * PIECE, PIECE), PIECE)
        copies.start(w_ref.at[:, col], ws.at[i, pl.ds(0, 512)])
        copies.start(rw_ref.at[:, col], ws.at[i, pl.ds(512, 512)])
    copies.wait(0, 3)
    for i, out in enumerate(outs):
        copies.wait(3 + 2 * i, 5 + 2 * i)
        out[...] = jnp.dot(
            ho[...], ws[i], preferred_element_type=jnp.float32
        ).astype(jnp.bfloat16)


SMEM = pl.BlockSpec(memory_space=pltpu.SMEM)
ANY = pl.BlockSpec(memory_space=pl.ANY)
VMEM = pl.BlockSpec(memory_space=pltpu.VMEM)


def key_scratch(keys):
    return [
        pltpu.VMEM((keys, HEAD_WIDTH), jnp.bfloat16),
        pltpu.VMEM((keys, 2 * HEAD_WIDTH), jnp.bfloat16),
    ]


STATE = [
    jax.ShapeDtypeStruct((HALF, 8 * HEAD_WIDTH), jnp.float32),
    jax.ShapeDtypeStruct((HALF, HEAD_WIDTH), jnp.float32),
]


def call(kernel, name, out_shape, scratch, keys, rows, args):
    return pl.pallas_call(
        kernel,
        out_shape=out_shape,
        in_specs=[SMEM, SMEM] + [ANY] * (len(args) - 2),
        out_specs=[VMEM] * len(out_shape),
        scratch_shapes=scratch,
        compiler_params=pltpu.CompilerParams(vmem_limit_bytes=GRANT),
        cost_estimate=pl.CostEstimate(
            flops=8 * rows * keys * 2 * HEAD_WIDTH * 2,
            bytes_accessed=4 * 2**20,
            transcendentals=8 * rows * keys,
        ),
        name=name,
    )(*args)


def near(*args):
    scratch = key_scratch(3 * SHARD) + [
        pltpu.VMEM((HALF, 1024), jnp.bfloat16),
        pltpu.VMEM((BLK, 3 * SHARD), jnp.float32),
        pltpu.SemaphoreType.DMA((8,)),
    ]
    return call(near_kernel, "near", STATE, scratch, 3 * SHARD, HALF, args)


def far(*args):
    scratch = key_scratch(6 * SHARD) + [
        pltpu.VMEM((HALF, 1024), jnp.bfloat16),
        pltpu.VMEM((2, 8, 6 * SHARD), jnp.float32),
        pltpu.VMEM((HALF, 1024), jnp.float32),
        pltpu.VMEM((HALF, HEAD_WIDTH), jnp.float32),
        pltpu.SemaphoreType.DMA((16,)),
    ]
    out = jax.ShapeDtypeStruct((HALF, 1024), jnp.bfloat16)
    return call(far_kernel, "far", [out], scratch, 6 * SHARD, HALF, args)[0]


def project(*args):
    out = jax.ShapeDtypeStruct((SHARD, PIECE), jnp.bfloat16)
    return pl.pallas_call(
        project_kernel,
        out_shape=[out] * 4,
        in_specs=[ANY] * 4,
        out_specs=[VMEM] * 4,
        scratch_shapes=[
            pltpu.VMEM((SHARD, 1024), jnp.bfloat16),
            pltpu.VMEM((4, 1024, PIECE), jnp.bfloat16),
            pltpu.SemaphoreType.DMA((11,)),
        ],
        compiler_params=pltpu.CompilerParams(vmem_limit_bytes=GRANT),
        cost_estimate=pl.CostEstimate(
            flops=10**9, bytes_accessed=4 * 2**20, transcendentals=0
        ),
        name="project",
    )(*args)


def f32_sum(*terms):
    return sum(t.astype(jnp.float32) for t in terms).astype(jnp.bfloat16)


def on_device(n_ctx, n_head, queries, key_rows, value_vectors, out_weight, doc_start, block_list):
    head = lax.axis_index("head")
    core = head % 2
    z = head // 2
    x = lax.axis_index("ctx") % X_CHIPS

    def go(block, route):
        return send(block, n_ctx, n_head, route)

    def pick(first, *arrays):
        return [jnp.where(first, a, b) for a, b in zip(arrays[:-1], arrays[1:])]

    own = jnp.concatenate(
        [
            lax.dynamic_index_in_dim(a, z, 1, keepdims=False)
            for a in (key_rows, value_vectors)
        ]
    )
    rq = go(queries, other_core)
    rw = go(out_weight, other_core)
    row_mine = go(own, to_later_rows(n_ctx))
    row_theirs = go(row_mine, other_core)
    four = jnp.where(core == 0, row_mine, row_theirs)
    eight = jnp.where(core == 0, row_theirs, row_mine)
    wraps = jnp.where(core == 0, x == X_CHIPS - 1, x >= 1)
    beside_load = jnp.concatenate(
        [jnp.where(wraps, four, own), jnp.where(wraps, eight, four)]
    )
    wraps = x >= X_CHIPS // 2
    across_load = jnp.where(
        core == 0, jnp.where(wraps, four, own), jnp.where(wraps, eight, four)
    )
    near_turn = go(beside_load, beside)
    far_turn = go(across_load, across)
    acc, ml = near(doc_start, block_list, queries, rq, own, row_mine, row_theirs)
    near_turn, far_turn, acc = lax.optimization_barrier((near_turn, far_turn, acc))
    turns = (
        near_turn, far_turn, go(near_turn, other_core), go(far_turn, other_core)
    )
    ho = far(doc_start, block_list, queries, rq, *turns, acc, ml)
    relay, plain, fwd, keep = project(ho, go(ho, other_core), out_weight, rw)
    came = go(relay, along_z(n_head))
    beyond = go(plain, along_z(n_head))
    summed = go(f32_sum(fwd, came), along_z(n_head))
    return f32_sum(keep, summed, go(beyond, other_core))


def solution(mesh):
    n_ctx, n_head = mesh.shape["ctx"], mesh.shape["head"]
    return jax.shard_map(
        functools.partial(on_device, n_ctx, n_head),
        mesh=mesh,
        in_specs=(
            P("ctx", "head"),
            P("ctx", None, None),
            P("ctx", None, None),
            P("head", None),
            P("ctx"),
            P("ctx", None),
        ),
        out_specs=P("ctx", "head"),
        check_vma=False,
    )
```

```python
import functools
import math

import jax
import jax.numpy as jnp
from jax import lax
from jax.experimental import pallas as pl
from jax.experimental.pallas import tpu as pltpu
from jax.sharding import PartitionSpec as P

HEAD_WIDTH = 128
BLK = 128
DOC_BLOCKS = 32
REACH = 8
SHARD = 512
HALF = 256
PIECE = 256
NEG = -1e30
EXP_SCALE = math.log2(math.e) / math.sqrt(HEAD_WIDTH)
AXES = ("ctx", "head")
X_CHIPS = 4
TURNS = (1, 3, 2)
GRANT = 40 * 2**20


def ctx_head_pairs(n_ctx, n_head, route):
    pairs = []
    for c in range(n_ctx):
        for h in range(n_head):
            target = route(c, h)
            if target is not None:
                pairs.append((c * n_head + h, target[0] * n_head + target[1]))
    return pairs


def send(block, n_ctx, n_head, route):
    return lax.ppermute(block, AXES, ctx_head_pairs(n_ctx, n_head, route))


def rows_on(n_ctx, shards):
    return lambda c, h: (c + shards, h) if c + shards < n_ctx else None


def turned(by):
    def route(c, h):
        return (c - c % X_CHIPS + (c + by) % X_CHIPS, h)

    return route


def other_core(c, h):
    return (c, h ^ 1)


def along_z(n_head):
    return lambda c, h: (c, (h + (2 if h % 2 == 0 else -2)) % n_head)


def dot_t(a, b):
    return lax.dot_general(
        a, b, (((1,), (1,)), ((), ())), preferred_element_type=jnp.float32
    )


def position():
    head = lax.axis_index("head")
    return lax.axis_index("ctx"), lax.div(head, 2), lax.rem(head, 2)


class Copies:
    def __init__(self, sem):
        self.sem, self.started = sem, []

    def start(self, src, dst):
        c = pltpu.make_async_copy(src, dst, self.sem.at[len(self.started)])
        c.start()
        self.started.append(c)

    def wait(self, first=0, last=None):
        for c in self.started[first:last]:
            c.wait()


def last_listed(list_ref):
    last = list_ref[0, 0]
    for i in range(1, list_ref.shape[1]):
        last = jnp.maximum(last, list_ref[0, i])
    return last


def block_range(doc_ref, list_ref, list_last, ctx, local):
    lo = jnp.maximum(doc_ref[local], list_ref[0, 0])
    hi = jnp.minimum(ctx * (SHARD // BLK) + local, list_last)
    return lo, hi


def write_bias(bias, ctx, distances, lo, hi):
    for j, d in enumerate(distances):
        block = (ctx - d) * (SHARD // BLK) + (
            lax.broadcasted_iota(jnp.int32, (bias.shape[0], SHARD), 1) // BLK
        )
        bias[:, j * SHARD : (j + 1) * SHARD] = jnp.where(
            (block >= lo) & (block <= hi), 0.0, NEG
        )


def load_shard(copies, mine, theirs, first, kx, vx, row, core):
    for ref, which in ((mine, core), (theirs, 1 - core)):
        at = pl.multiple_of(row + which * HALF, HALF)
        copies.start(ref.at[pl.ds(first, HALF)], kx.at[pl.ds(at, HALF)])
        copies.start(
            ref.at[pl.ds(first + HALF, HALF)],
            vx.at[pl.ds(at, HALF), pl.ds(0, HEAD_WIDTH)],
        )


def softmax_tile(q, k, v, mask, m, acc):
    s = dot_t(q, k) + mask
    top = jnp.max(s, axis=1, keepdims=True)
    m_new = top if m is None else jnp.maximum(m, top)
    p = jnp.exp2((s - m_new) * EXP_SCALE).astype(jnp.bfloat16)
    pv = jnp.dot(p, v, preferred_element_type=jnp.float32)
    if m is not None:
        pv = acc * jnp.exp2((m - m_new) * EXP_SCALE) + pv
    return m_new, pv


def head_columns(g):
    return slice(g * HEAD_WIDTH, (g + 1) * HEAD_WIDTH)


def load_queries(copies, q_ref, rq_ref, row, rows, qs):
    at = pl.multiple_of(row, BLK)
    copies.start(q_ref.at[pl.ds(at, rows)], qs.at[:, pl.ds(0, 512)])
    copies.start(rq_ref.at[pl.ds(at, rows)], qs.at[:, pl.ds(512, 512)])


def near_kernel(doc_ref, list_ref, q_ref, rq_ref, k_ref, v_ref, *rest):
    four, eight, their_four, their_eight = rest[:4]
    rest = rest[4:]
    acc_ref, ml_ref, kx, vx, qs, mask, sem = rest
    ctx, z, core = position()
    copies = Copies(sem)
    load_queries(copies, q_ref, rq_ref, core * HALF, HALF, qs)
    copies.start(k_ref, kx.at[pl.ds(0, SHARD)])
    copies.start(v_ref, vx.at[pl.ds(0, SHARD), pl.ds(0, HEAD_WIDTH)])
    load_shard(copies, four, their_four, 0, kx, vx, SHARD, core)
    load_shard(copies, eight, their_eight, 0, kx, vx, 2 * SHARD, core)
    vx[:, HEAD_WIDTH:] = jnp.ones((vx.shape[0], HEAD_WIDTH), jnp.bfloat16)
    lane = lax.broadcasted_iota(jnp.int32, (BLK, HEAD_WIDTH), 1)
    list_last = last_listed(list_ref)

    def write_mask(ii):
        local = core * 2 + ii
        lo, hi = block_range(doc_ref, list_ref, list_last, ctx, local)
        write_bias(mask, ctx, (0, 4, 8), lo, hi)
        col = lax.broadcasted_iota(jnp.int32, (BLK, SHARD), 1)
        at = lax.broadcasted_iota(jnp.int32, (BLK, SHARD), 0) + local * BLK
        mask[:, :SHARD] = jnp.where(col <= at, mask[:, :SHARD], NEG)

    def block(ii, carry):
        rows = pl.ds(pl.multiple_of(ii * BLK, BLK), BLK)
        ml = jnp.zeros((BLK, HEAD_WIDTH), jnp.float32)
        for g in range(8):
            q = qs[rows, head_columns(g)]
            m, acc = softmax_tile(q, kx[...], vx[...], mask[...], None, None)
            acc_ref[rows, head_columns(g)] = acc[:, :HEAD_WIDTH]
            ml = jnp.where(lane == g, m, ml)
            ml = jnp.where(lane == 8 + g, acc[:, HEAD_WIDTH:], ml)
        ml_ref[rows, :] = ml

        @pl.when(ii == 0)
        def _():
            write_mask(1)

        return carry

    write_mask(0)
    copies.wait()
    lax.fori_loop(0, 2, block, 0)


def joined(acc_ref, ml_ref, rows, g):
    l_in = jnp.broadcast_to(ml_ref[rows, 8 + g : 9 + g], (BLK, HEAD_WIDTH))
    acc = jnp.concatenate([acc_ref[rows, head_columns(g)], l_in], axis=1)
    return ml_ref[rows, g : g + 1], acc


def far_kernel(doc_ref, list_ref, q_ref, rq_ref, *rest):
    mine, theirs, (acc_in, ml_in, ho) = rest[:3], rest[3:6], rest[6:9]
    kx, vx, qs, bias, acc_s, ml_s, sem = rest[9:]
    ctx, z, core = position()
    copies = Copies(sem)
    distances = []
    for by, a, b in zip(TURNS, mine, theirs):
        for part in range(2):
            at = len(distances) * SHARD
            load_shard(copies, a, b, part * SHARD, kx, vx, at, core)
            distances.append(by + 4 * part)
    load_queries(copies, q_ref, rq_ref, core * HALF, HALF, qs)
    copies.start(acc_in, acc_s)
    copies.start(ml_in, ml_s)
    vx[:, HEAD_WIDTH:] = jnp.ones((vx.shape[0], HEAD_WIDTH), jnp.bfloat16)
    list_last = last_listed(list_ref)
    for ii in range(2):
        lo, hi = block_range(doc_ref, list_ref, list_last, ctx, core * 2 + ii)
        write_bias(bias.at[ii], ctx, distances, lo, hi)
    copies.wait()

    def block(ii, carry):
        rows = pl.ds(pl.multiple_of(ii * BLK, BLK), BLK)
        for g in range(8):
            q = qs[rows, head_columns(g)]
            m, acc = joined(acc_s, ml_s, rows, g)
            _, acc = softmax_tile(q, kx[...], vx[...], bias[ii, 0:1, :], m, acc)
            o = acc[:, :HEAD_WIDTH] / acc[:, HEAD_WIDTH:]
            ho[rows, head_columns(g)] = o.astype(jnp.bfloat16)
        return carry

    lax.fori_loop(0, 2, block, 0)

def project_kernel(ho_ref, got_ref, w_ref, rw_ref, *rest):
    outs = rest[:4]
    ho, ws, sem = rest[4:]
    ctx, z, core = position()
    copies = Copies(sem)
    dz = jnp.where(core == 0, 1, 3)
    wanted = ((2, core), (dz, 1 - core), (dz, core), (0, core))
    mine = pl.ds(pl.multiple_of(core * HALF, HALF), HALF)
    theirs = pl.ds(pl.multiple_of((1 - core) * HALF, HALF), HALF)
    copies.start(ho_ref, ho.at[mine])
    copies.start(got_ref.at[:, pl.ds(0, 512)], ho.at[theirs, pl.ds(512, 512)])
    copies.start(got_ref.at[:, pl.ds(512, 512)], ho.at[theirs, pl.ds(0, 512)])
    for i, (away, part) in enumerate(wanted):
        target = lax.rem(z + away, 4) * 2 + part
        col = pl.ds(pl.multiple_of(target * PIECE, PIECE), PIECE)
        copies.start(w_ref.at[:, col], ws.at[i, pl.ds(0, 512)])
        copies.start(rw_ref.at[:, col], ws.at[i, pl.ds(512, 512)])
    copies.wait(0, 3)
    for i, out in enumerate(outs):
        copies.wait(3 + 2 * i, 5 + 2 * i)
        out[...] = jnp.dot(
            ho[...], ws[i], preferred_element_type=jnp.float32
        ).astype(jnp.bfloat16)


SMEM = pl.BlockSpec(memory_space=pltpu.SMEM)
ANY = pl.BlockSpec(memory_space=pl.ANY)
VMEM = pl.BlockSpec(memory_space=pltpu.VMEM)


def key_scratch(keys):
    return [
        pltpu.VMEM((keys, HEAD_WIDTH), jnp.bfloat16),
        pltpu.VMEM((keys, 2 * HEAD_WIDTH), jnp.bfloat16),
    ]


STATE = [
    jax.ShapeDtypeStruct((HALF, 8 * HEAD_WIDTH), jnp.float32),
    jax.ShapeDtypeStruct((HALF, HEAD_WIDTH), jnp.float32),
]


def call(kernel, name, out_shape, scratch, keys, rows, args):
    return pl.pallas_call(
        kernel,
        out_shape=out_shape,
        in_specs=[SMEM, SMEM] + [ANY] * (len(args) - 2),
        out_specs=[VMEM] * len(out_shape),
        scratch_shapes=scratch,
        compiler_params=pltpu.CompilerParams(vmem_limit_bytes=GRANT),
        cost_estimate=pl.CostEstimate(
            flops=8 * rows * keys * 2 * HEAD_WIDTH * 2,
            bytes_accessed=4 * 2**20,
            transcendentals=8 * rows * keys,
        ),
        name=name,
    )(*args)


def near(*args):
    scratch = key_scratch(3 * SHARD) + [
        pltpu.VMEM((HALF, 1024), jnp.bfloat16),
        pltpu.VMEM((BLK, 3 * SHARD), jnp.float32),
        pltpu.SemaphoreType.DMA((12,)),
    ]
    return call(near_kernel, "near", STATE, scratch, 3 * SHARD, HALF, args)


def far(*args):
    scratch = key_scratch(6 * SHARD) + [
        pltpu.VMEM((HALF, 1024), jnp.bfloat16),
        pltpu.VMEM((2, 8, 6 * SHARD), jnp.float32),
        pltpu.VMEM((HALF, 1024), jnp.float32),
        pltpu.VMEM((HALF, HEAD_WIDTH), jnp.float32),
        pltpu.SemaphoreType.DMA((28,)),
    ]
    out = jax.ShapeDtypeStruct((HALF, 1024), jnp.bfloat16)
    return call(far_kernel, "far", [out], scratch, 6 * SHARD, HALF, args)[0]


def project(*args):
    out = jax.ShapeDtypeStruct((SHARD, PIECE), jnp.bfloat16)
    return pl.pallas_call(
        project_kernel,
        out_shape=[out] * 4,
        in_specs=[ANY] * 4,
        out_specs=[VMEM] * 4,
        scratch_shapes=[
            pltpu.VMEM((SHARD, 1024), jnp.bfloat16),
            pltpu.VMEM((4, 1024, PIECE), jnp.bfloat16),
            pltpu.SemaphoreType.DMA((11,)),
        ],
        compiler_params=pltpu.CompilerParams(vmem_limit_bytes=GRANT),
        cost_estimate=pl.CostEstimate(
            flops=10**9, bytes_accessed=4 * 2**20, transcendentals=0
        ),
        name="project",
    )(*args)


def f32_sum(*terms):
    return sum(t.astype(jnp.float32) for t in terms).astype(jnp.bfloat16)


def on_device(n_ctx, n_head, queries, key_rows, value_vectors, out_weight, doc_start, block_list):
    head = lax.axis_index("head")
    core = head % 2
    z = head // 2
    x = lax.axis_index("ctx") % X_CHIPS

    def go(block, route):
        return send(block, n_ctx, n_head, route)

    own_k, own_v = (
        lax.dynamic_index_in_dim(a, z, 1, keepdims=False)
        for a in (key_rows, value_vectors)
    )
    own = jnp.concatenate(
        [lax.dynamic_slice_in_dim(a, core * HALF, HALF, 0) for a in (own_k, own_v)]
    )
    rq = go(queries, other_core)
    rw = go(out_weight, other_core)
    four = go(own, rows_on(n_ctx, 4))
    eight = go(own, rows_on(n_ctx, 8))
    loads = []
    for by in TURNS:
        wraps = x + by >= X_CHIPS
        loads.append(
            jnp.concatenate(
                [jnp.where(wraps, four, own), jnp.where(wraps, eight, four)]
            )
        )
    *loads, own_k = lax.optimization_barrier((*loads, own_k))
    turns = [go(load, turned(by)) for load, by in zip(loads, TURNS)]
    acc, ml = near(
        doc_start, block_list, queries, rq, own_k, own_v,
        four, eight, go(four, other_core), go(eight, other_core),
    )
    *turns, acc = lax.optimization_barrier((*turns, acc))
    turns += [go(t, other_core) for t in turns]
    ho = far(doc_start, block_list, queries, rq, *turns, acc, ml)
    relay, plain, fwd, keep = project(ho, go(ho, other_core), out_weight, rw)
    came = go(relay, along_z(n_head))
    beyond = go(plain, along_z(n_head))
    summed = go(f32_sum(fwd, came), along_z(n_head))
    return f32_sum(keep, summed, go(beyond, other_core))


def solution(mesh):
    n_ctx, n_head = mesh.shape["ctx"], mesh.shape["head"]
    return jax.shard_map(
        functools.partial(on_device, n_ctx, n_head),
        mesh=mesh,
        in_specs=(
            P("ctx", "head"),
            P("ctx", None, None),
            P("ctx", None, None),
            P("head", None),
            P("ctx"),
            P("ctx", None),
        ),
        out_specs=P("ctx", "head"),
        check_vma=False,
    )
```

```python
import functools
import math

import jax
import jax.numpy as jnp
from jax import lax
from jax.experimental import pallas as pl
from jax.experimental.pallas import tpu as pltpu
from jax.sharding import PartitionSpec as P

HEAD_WIDTH = 128
BLK = 128
DOC_BLOCKS = 32
REACH = 8
SHARD = 512
HALF = 256
PIECE = 256
NEG = -1e30
EXP_SCALE = math.log2(math.e) / math.sqrt(HEAD_WIDTH)
AXES = ("ctx", "head")
X_CHIPS = 4
TURNS = (1, 3, 2)
GRANT = 40 * 2**20


def ctx_head_pairs(n_ctx, n_head, route):
    pairs = []
    for c in range(n_ctx):
        for h in range(n_head):
            target = route(c, h)
            if target is not None:
                pairs.append((c * n_head + h, target[0] * n_head + target[1]))
    return pairs


def send(block, n_ctx, n_head, route):
    return lax.ppermute(block, AXES, ctx_head_pairs(n_ctx, n_head, route))


def rows_on(n_ctx, shards):
    return lambda c, h: (c + shards, h) if c + shards < n_ctx else None


def turned(by):
    def route(c, h):
        return (c - c % X_CHIPS + (c + by) % X_CHIPS, h)

    return route


def other_core(c, h):
    return (c, h ^ 1)


def along_z(n_head):
    return lambda c, h: (c, (h + (2 if h % 2 == 0 else -2)) % n_head)


def dot_t(a, b):
    return lax.dot_general(
        a, b, (((1,), (1,)), ((), ())), preferred_element_type=jnp.float32
    )


def position():
    head = lax.axis_index("head")
    return lax.axis_index("ctx"), lax.div(head, 2), lax.rem(head, 2)


class Copies:
    def __init__(self, sem):
        self.sem, self.started = sem, []

    def start(self, src, dst):
        c = pltpu.make_async_copy(src, dst, self.sem.at[len(self.started)])
        c.start()
        self.started.append(c)

    def wait(self, first=0, last=None):
        for c in self.started[first:last]:
            c.wait()


def last_listed(list_ref):
    last = list_ref[0, 0]
    for i in range(1, list_ref.shape[1]):
        last = jnp.maximum(last, list_ref[0, i])
    return last


def block_range(doc_ref, list_ref, list_last, ctx, local):
    lo = jnp.maximum(doc_ref[local], list_ref[0, 0])
    hi = jnp.minimum(ctx * (SHARD // BLK) + local, list_last)
    return lo, hi


def write_bias(bias, ctx, distances, lo, hi):
    for j, d in enumerate(distances):
        block = (ctx - d) * (SHARD // BLK) + (
            lax.broadcasted_iota(jnp.int32, (bias.shape[0], SHARD), 1) // BLK
        )
        bias[:, j * SHARD : (j + 1) * SHARD] = jnp.where(
            (block >= lo) & (block <= hi), 0.0, NEG
        )


def load_shard(copies, mine, theirs, first, kx, vx, row, core):
    for ref, which in ((mine, core), (theirs, 1 - core)):
        at = pl.multiple_of(row + which * HALF, HALF)
        copies.start(ref.at[pl.ds(first, HALF)], kx.at[pl.ds(at, HALF)])
        copies.start(
            ref.at[pl.ds(first + HALF, HALF)],
            vx.at[pl.ds(at, HALF), pl.ds(0, HEAD_WIDTH)],
        )


def softmax_tile(q, k, v, mask, m, acc):
    s = dot_t(q, k) + mask
    top = jnp.max(s, axis=1, keepdims=True)
    m_new = top if m is None else jnp.maximum(m, top)
    p = jnp.exp2((s - m_new) * EXP_SCALE).astype(jnp.bfloat16)
    pv = jnp.dot(p, v, preferred_element_type=jnp.float32)
    if m is not None:
        pv = acc * jnp.exp2((m - m_new) * EXP_SCALE) + pv
    return m_new, pv


def head_columns(g):
    return slice(g * HEAD_WIDTH, (g + 1) * HEAD_WIDTH)


def load_queries(copies, q_ref, rq_ref, row, rows, qs):
    at = pl.multiple_of(row, BLK)
    copies.start(q_ref.at[pl.ds(at, rows)], qs.at[:, pl.ds(0, 512)])
    copies.start(rq_ref.at[pl.ds(at, rows)], qs.at[:, pl.ds(512, 512)])


def near_kernel(doc_ref, list_ref, q_ref, rq_ref, k_ref, v_ref, *rest):
    four, eight, their_four, their_eight = rest[:4]
    rest = rest[4:]
    acc_ref, ml_ref, kx, vx, qs, mask, sem = rest
    ctx, z, core = position()
    copies = Copies(sem)
    load_queries(copies, q_ref, rq_ref, core * HALF, HALF, qs)
    copies.start(k_ref, kx.at[pl.ds(0, SHARD)])
    copies.start(v_ref, vx.at[pl.ds(0, SHARD), pl.ds(0, HEAD_WIDTH)])
    load_shard(copies, four, their_four, 0, kx, vx, SHARD, core)
    load_shard(copies, eight, their_eight, 0, kx, vx, 2 * SHARD, core)
    vx[:, HEAD_WIDTH:] = jnp.ones((vx.shape[0], HEAD_WIDTH), jnp.bfloat16)
    lane = lax.broadcasted_iota(jnp.int32, (BLK, HEAD_WIDTH), 1)
    list_last = last_listed(list_ref)

    def write_mask(ii):
        local = core * 2 + ii
        lo, hi = block_range(doc_ref, list_ref, list_last, ctx, local)
        write_bias(mask, ctx, (0, 4, 8), lo, hi)
        col = lax.broadcasted_iota(jnp.int32, (BLK, SHARD), 1)
        at = lax.broadcasted_iota(jnp.int32, (BLK, SHARD), 0) + local * BLK
        mask[:, :SHARD] = jnp.where(col <= at, mask[:, :SHARD], NEG)

    def block(ii, carry):
        rows = pl.ds(pl.multiple_of(ii * BLK, BLK), BLK)
        ml = jnp.zeros((BLK, HEAD_WIDTH), jnp.float32)
        for g in range(8):
            q = qs[rows, head_columns(g)]
            m, acc = softmax_tile(q, kx[...], vx[...], mask[...], None, None)
            acc_ref[rows, head_columns(g)] = acc[:, :HEAD_WIDTH]
            ml = jnp.where(lane == g, m, ml)
            ml = jnp.where(lane == 8 + g, acc[:, HEAD_WIDTH:], ml)
        ml_ref[rows, :] = ml

        @pl.when(ii == 0)
        def _():
            write_mask(1)

        return carry

    write_mask(0)
    copies.wait()
    lax.fori_loop(0, 2, block, 0)


def joined(acc_ref, ml_ref, rows, g):
    l_in = jnp.broadcast_to(ml_ref[rows, 8 + g : 9 + g], (BLK, HEAD_WIDTH))
    acc = jnp.concatenate([acc_ref[rows, head_columns(g)], l_in], axis=1)
    return ml_ref[rows, g : g + 1], acc


def far_kernel(doc_ref, list_ref, q_ref, rq_ref, *rest):
    mine, theirs, (acc_in, ml_in, ho) = rest[:3], rest[3:6], rest[6:9]
    kx, vx, qs, bias, acc_s, ml_s, sem = rest[9:]
    ctx, z, core = position()
    copies = Copies(sem)
    distances = []
    for by, a, b in zip(TURNS, mine, theirs):
        for part in range(2):
            at = len(distances) * SHARD
            load_shard(copies, a, b, part * SHARD, kx, vx, at, core)
            distances.append(by + 4 * part)
    load_queries(copies, q_ref, rq_ref, core * HALF, HALF, qs)
    copies.start(acc_in, acc_s)
    copies.start(ml_in, ml_s)
    vx[:, HEAD_WIDTH:] = jnp.ones((vx.shape[0], HEAD_WIDTH), jnp.bfloat16)
    list_last = last_listed(list_ref)
    for ii in range(2):
        lo, hi = block_range(doc_ref, list_ref, list_last, ctx, core * 2 + ii)
        write_bias(bias.at[ii], ctx, distances, lo, hi)
    copies.wait()

    def block(ii, carry):
        rows = pl.ds(pl.multiple_of(ii * BLK, BLK), BLK)
        for g in range(8):
            q = qs[rows, head_columns(g)]
            m, acc = joined(acc_s, ml_s, rows, g)
            _, acc = softmax_tile(q, kx[...], vx[...], bias[ii, 0:1, :], m, acc)
            o = acc[:, :HEAD_WIDTH] / acc[:, HEAD_WIDTH:]
            ho[rows, head_columns(g)] = o.astype(jnp.bfloat16)
        return carry

    lax.fori_loop(0, 2, block, 0)

def project_kernel(first, last, ho_ref, got_ref, w_ref, rw_ref, *rest):
    outs = rest[: last - first]
    ho, ws, sem = rest[last - first :]
    ctx, z, core = position()
    copies = Copies(sem)
    dz = jnp.where(core == 0, 1, 3)
    wanted = ((2, core), (dz, 1 - core), (dz, core), (0, core))[first:last]
    mine = pl.ds(pl.multiple_of(core * HALF, HALF), HALF)
    theirs = pl.ds(pl.multiple_of((1 - core) * HALF, HALF), HALF)
    copies.start(ho_ref, ho.at[mine])
    copies.start(got_ref.at[:, pl.ds(0, 512)], ho.at[theirs, pl.ds(512, 512)])
    copies.start(got_ref.at[:, pl.ds(512, 512)], ho.at[theirs, pl.ds(0, 512)])
    for i, (away, part) in enumerate(wanted):
        target = lax.rem(z + away, 4) * 2 + part
        col = pl.ds(pl.multiple_of(target * PIECE, PIECE), PIECE)
        copies.start(w_ref.at[:, col], ws.at[i, pl.ds(0, 512)])
        copies.start(rw_ref.at[:, col], ws.at[i, pl.ds(512, 512)])
    copies.wait(0, 3)
    for i, out in enumerate(outs):
        copies.wait(3 + 2 * i, 5 + 2 * i)
        out[...] = jnp.dot(
            ho[...], ws[i], preferred_element_type=jnp.float32
        ).astype(jnp.bfloat16)


SMEM = pl.BlockSpec(memory_space=pltpu.SMEM)
ANY = pl.BlockSpec(memory_space=pl.ANY)
VMEM = pl.BlockSpec(memory_space=pltpu.VMEM)


def key_scratch(keys):
    return [
        pltpu.VMEM((keys, HEAD_WIDTH), jnp.bfloat16),
        pltpu.VMEM((keys, 2 * HEAD_WIDTH), jnp.bfloat16),
    ]


STATE = [
    jax.ShapeDtypeStruct((HALF, 8 * HEAD_WIDTH), jnp.float32),
    jax.ShapeDtypeStruct((HALF, HEAD_WIDTH), jnp.float32),
]


def call(kernel, name, out_shape, scratch, keys, rows, args):
    return pl.pallas_call(
        kernel,
        out_shape=out_shape,
        in_specs=[SMEM, SMEM] + [ANY] * (len(args) - 2),
        out_specs=[VMEM] * len(out_shape),
        scratch_shapes=scratch,
        compiler_params=pltpu.CompilerParams(vmem_limit_bytes=GRANT),
        cost_estimate=pl.CostEstimate(
            flops=8 * rows * keys * 2 * HEAD_WIDTH * 2,
            bytes_accessed=4 * 2**20,
            transcendentals=8 * rows * keys,
        ),
        name=name,
    )(*args)


def near(*args):
    scratch = key_scratch(3 * SHARD) + [
        pltpu.VMEM((HALF, 1024), jnp.bfloat16),
        pltpu.VMEM((BLK, 3 * SHARD), jnp.float32),
        pltpu.SemaphoreType.DMA((12,)),
    ]
    return call(near_kernel, "near", STATE, scratch, 3 * SHARD, HALF, args)


def far(*args):
    scratch = key_scratch(6 * SHARD) + [
        pltpu.VMEM((HALF, 1024), jnp.bfloat16),
        pltpu.VMEM((2, 8, 6 * SHARD), jnp.float32),
        pltpu.VMEM((HALF, 1024), jnp.float32),
        pltpu.VMEM((HALF, HEAD_WIDTH), jnp.float32),
        pltpu.SemaphoreType.DMA((28,)),
    ]
    out = jax.ShapeDtypeStruct((HALF, 1024), jnp.bfloat16)
    return call(far_kernel, "far", [out], scratch, 6 * SHARD, HALF, args)[0]


def project(first, last, *args):
    count = last - first
    out = jax.ShapeDtypeStruct((SHARD, PIECE), jnp.bfloat16)
    return pl.pallas_call(
        functools.partial(project_kernel, first, last),
        out_shape=[out] * count,
        in_specs=[ANY] * 4,
        out_specs=[VMEM] * count,
        scratch_shapes=[
            pltpu.VMEM((SHARD, 1024), jnp.bfloat16),
            pltpu.VMEM((count, 1024, PIECE), jnp.bfloat16),
            pltpu.SemaphoreType.DMA((3 + 2 * count,)),
        ],
        compiler_params=pltpu.CompilerParams(vmem_limit_bytes=GRANT),
        cost_estimate=pl.CostEstimate(
            flops=count * 2**28, bytes_accessed=count * 2**20, transcendentals=0
        ),
        name=f"project{first}",
    )(*args)


def f32_sum(*terms):
    return sum(t.astype(jnp.float32) for t in terms).astype(jnp.bfloat16)


def on_device(n_ctx, n_head, queries, key_rows, value_vectors, out_weight, doc_start, block_list):
    head = lax.axis_index("head")
    core = head % 2
    z = head // 2
    x = lax.axis_index("ctx") % X_CHIPS

    def go(block, route):
        return send(block, n_ctx, n_head, route)

    own_k, own_v = (
        lax.dynamic_index_in_dim(a, z, 1, keepdims=False)
        for a in (key_rows, value_vectors)
    )
    own = jnp.concatenate(
        [lax.dynamic_slice_in_dim(a, core * HALF, HALF, 0) for a in (own_k, own_v)]
    )
    rq = go(queries, other_core)
    rw = go(out_weight, other_core)
    four = go(own, rows_on(n_ctx, 4))
    eight = go(own, rows_on(n_ctx, 8))
    loads = []
    for by in TURNS:
        wraps = x + by >= X_CHIPS
        loads.append(
            jnp.concatenate(
                [jnp.where(wraps, four, own), jnp.where(wraps, eight, four)]
            )
        )
    *loads, own_k = lax.optimization_barrier((*loads, own_k))
    turns = [go(load, turned(by)) for load, by in zip(loads, TURNS)]
    acc, ml = near(
        doc_start, block_list, queries, rq, own_k, own_v,
        four, eight, go(four, other_core), go(eight, other_core),
    )
    *turns, acc = lax.optimization_barrier((*turns, acc))
    turns += [go(t, other_core) for t in turns]
    ho = far(doc_start, block_list, queries, rq, *turns, acc, ml)
    got = go(ho, other_core)
    relay, plain = project(0, 2, ho, got, out_weight, rw)
    relay, plain, got = lax.optimization_barrier((relay, plain, got))
    came = go(relay, along_z(n_head))
    fwd, keep = project(2, 4, ho, got, out_weight, rw)
    beyond = go(plain, along_z(n_head))
    summed = go(f32_sum(fwd, came), along_z(n_head))
    return f32_sum(keep, summed, go(beyond, other_core))


def solution(mesh):
    n_ctx, n_head = mesh.shape["ctx"], mesh.shape["head"]
    return jax.shard_map(
        functools.partial(on_device, n_ctx, n_head),
        mesh=mesh,
        in_specs=(
            P("ctx", "head"),
            P("ctx", None, None),
            P("ctx", None, None),
            P("head", None),
            P("ctx"),
            P("ctx", None),
        ),
        out_specs=P("ctx", "head"),
        check_vma=False,
    )
```
